32 devices in a mesh: seq: 16 (over z, y, core), chan: 2 (over x).
Axes of the slice: x: 2, y: 2, z: 4, core: 2. Of those that a mesh axis runs over, the one named last changes fastest.
Arguments:
- tokens: bfloat16 [2048, 4096], P('seq', 'chan'), may hold values from -6 to 6
- w_in: bfloat16 [4096, 3, 2048], P(None, None, 'chan'), may hold values from -0.09375 to 0.09375
- short_taps: float32 [3, 3, 2048], P(None, None, 'chan'), may hold values from -3 to 3
- skip_gain: float32 [2048], P('chan'), may hold values from 0.5 to 1.5
- filters: float32 [128, 2048], P('chan'), may hold values from -4 to 4
- w_out: bfloat16 [2048, 4096], P('chan'), may hold values from -0.125 to 0.125
Outputs:
- mixed: bfloat16 [2048, 4096], P('seq', 'chan')
The draws below stay inside these ranges and needn't reach their ends.
All inputs are finite; a program needn't handle non-finite values.
Results may differ from the reference program's by a relative error of at most 0.015.
Values may be sent and summed in bfloat16 or wider, within the bound.
A program may use at most 128 MiB of HBM per device.

```python
import jax
import jax.numpy as jnp
from jax import lax

D = 4096
C = 2048
GS = 16
G = 128
TOKENS = 2048
N_CHAN = 2


def draw_filters(key, part):
    keys = jax.random.split(key, 6)
    length = TOKENS
    steps = jnp.arange(length, dtype=jnp.float32)[None, :]
    slow = jax.random.randint(keys[0], (G, 1), 0, 10) < 5
    slow_rate = jnp.exp(jax.random.uniform(keys[1], (G, 1), jnp.float32, jnp.log(0.2 / length), jnp.log(1.0 / length)))
    fast_rate = jnp.exp(jax.random.uniform(keys[2], (G, 1), jnp.float32, jnp.log(1.0 / 50.0), jnp.log(1.0 / 30.0)))
    rate = jnp.where(slow, slow_rate, fast_rate)
    places = jax.random.randint(keys[3], (G, 4), 0, length)
    factors = jax.random.uniform(keys[4], (G, 4), jnp.float32, 0.5, 0.8)
    passed = (steps[:, None, :] >= places[:, :, None].astype(jnp.float32)).astype(jnp.float32)
    losses = jnp.sum(jnp.log(factors)[:, :, None] * passed, axis=1)
    envelope = jnp.exp(-rate * steps + losses)
    envelope = envelope / jnp.sqrt(jnp.sum(envelope * envelope, axis=1, keepdims=True))
    noise = jnp.clip(jax.random.normal(keys[5], (G, length), jnp.float32), -4.0, 4.0)
    return (envelope * noise).astype(jnp.float32)


def steps_of(rng, extent, pieces, least, top_value):
    gain, own = 1.0, jax.random.fold_in(rng, 6)
    for position, shards_of in pieces:
        heights = jnp.exp(jax.random.uniform(jax.random.fold_in(own, position), (shards_of,), jnp.float32, least / len(pieces), top_value / len(pieces)))
        gain = gain * jnp.repeat(heights, extent[position] // shards_of).reshape([-1 if axis == position else 1 for axis in range(len(extent))])
    return gain


def centred(stream_key, extent, deviation, bound, shards=(), kind=jnp.bfloat16):
    drawn = deviation * jax.random.normal(stream_key, extent, jnp.float32)
    if shards:
        drawn = drawn * steps_of(stream_key, extent, shards, -0.22, 0.18)
    return jnp.clip(drawn, -bound, bound).astype(kind)


def setup_inputs(seed: int = 0) -> dict:
    streams_of = jax.random.split(jax.random.key(seed), 7)
    return {
        "tokens": centred(streams_of[0], (TOKENS, D), 1.0, 6.0, ((0, 16), (1, 2))),
        "w_in": centred(streams_of[1], (D, 3, C), D ** -0.5, 0.09375, ((2, 2),)),
        "short_taps": centred(streams_of[2], (3, 3, C), 0.6, 3.0, ((2, 2),), jnp.float32),
        "skip_gain": jnp.clip(0.5 + 1.0 * jax.random.uniform(streams_of[3], (C,), jnp.float32) ** steps_of(streams_of[3], (C,), ((0, 2),), -0.2, 0.2), 0.5, 1.5),
        "filters": draw_filters(jax.random.fold_in(streams_of[6], 71), 0),
        "w_out": centred(streams_of[5], (C, D), C ** -0.5, 0.125, ((0, 2),)),
    }


def add_block(total, pair):
    part = jnp.dot(pair[0], pair[1], preferred_element_type=jnp.float32).astype(jnp.bfloat16)
    part = lax.optimization_barrier(part).astype(jnp.float32)
    return total + part, None


def reference(tokens, w_in, short_taps, skip_gain, filters, w_out):
    proj = jnp.dot(tokens, w_in.reshape(D, 3 * C), preferred_element_type=jnp.float32)
    proj = proj.astype(jnp.bfloat16).reshape(TOKENS, 3, C).astype(jnp.float32)
    padded = jnp.pad(proj, ((2, 0), (0, 0), (0, 0)))
    streams = short_taps[0] * padded[2:2 + TOKENS]
    streams = streams + short_taps[1] * padded[1:1 + TOKENS]
    streams = streams + short_taps[2] * padded[0:TOKENS]
    gated = (streams[:, 1, :] * streams[:, 2, :]).astype(jnp.bfloat16)
    taps = filters.astype(jnp.bfloat16).astype(jnp.float32)
    per_channel = jnp.repeat(taps, GS, axis=0).T
    length = 2 * TOKENS
    gated_wide = gated.astype(jnp.float32)
    spectrum = jnp.fft.rfft(gated_wide, length, axis=0) * jnp.fft.rfft(per_channel, length, axis=0)
    long_out = jnp.fft.irfft(spectrum, length, axis=0)[:TOKENS].astype(jnp.float32)
    long_out = long_out + skip_gain * gated_wide
    mixer = (streams[:, 0, :] * long_out).astype(jnp.bfloat16)
    mixer_blocks = mixer.reshape(TOKENS, N_CHAN, C // N_CHAN).transpose(1, 0, 2)
    weight_blocks = w_out.reshape(N_CHAN, C // N_CHAN, D)
    total, unused = lax.scan(add_block, jnp.zeros((TOKENS, D), jnp.float32), (mixer_blocks, weight_blocks))
    return total.astype(jnp.bfloat16)
```

```python
import functools

import jax
import jax.numpy as jnp
from jax import lax
from jax.experimental import pallas as pl
from jax.experimental.pallas import tpu as pltpu
from jax.sharding import PartitionSpec as P

MESH = pl.DeviceIdType.MESH
BF = jnp.bfloat16
F32 = jnp.float32
LANES = 128
HALO = 8


def dot(a, b):
    return jnp.dot(a, b, preferred_element_type=F32)


def kernel(
    n_seq, n_chan, piece, padded, gs, fc,
    tokens, taps, skip, filters, w_in, w_out,
    out,
    wv, wov, xt, acc, ext, gated, first, toep, zs, zr, ys, lr, hs, hr, ps, pr,
    w_sem, wo_sem, xs_sem, xr_sem, h_sem, z_send, z_recv, y_send, y_recv, p_send, p_recv,
):
    rows, feats = tokens.shape
    width = wv.shape[3]
    parts = feats // fc
    seq, chan = lax.axis_index("seq"), lax.axis_index("chan")

    loads = {}
    for d in range(n_chan):
        source = lax.rem(chan - d + n_chan, n_chan)
        for k in range(parts):
            start = pl.multiple_of(source * feats + k * fc, fc)
            loads[d, k] = pltpu.make_async_copy(
                w_in.at[:, pl.ds(start, fc), :],
                wv.at[d, :, pl.ds(k * fc, fc), :],
                w_sem.at[d, k],
            )
            loads[d, k].start()
    out_loads = {}
    for d in list(range(1, n_chan)) + [0]:
        target = lax.rem(chan + d, n_chan)
        start = pl.multiple_of(target * feats, feats)
        out_loads[d] = pltpu.make_async_copy(
            w_out.at[:, pl.ds(start, feats)], wov.at[d], wo_sem.at[d]
        )
        out_loads[d].start()

    barrier = pltpu.get_barrier_semaphore()
    for d in range(1, n_chan):
        pl.semaphore_signal(
            barrier, inc=1, device_id={"chan": lax.rem(chan + d, n_chan)}, device_id_type=MESH
        )
    for d in range(1, n_seq):
        pl.semaphore_signal(
            barrier, inc=1, device_id={"seq": lax.rem(seq + d, n_seq)}, device_id_type=MESH
        )
    pl.semaphore_wait(barrier, n_chan - 1 + n_seq - 1)

    token_sends = {}
    for k in range(parts):
        for d in range(1, n_chan):
            token_sends[d, k] = pltpu.make_async_remote_copy(
                src_ref=tokens.at[:, pl.ds(k * fc, fc)],
                dst_ref=xt.at[d - 1, :, pl.ds(k * fc, fc)],
                send_sem=xs_sem.at[d - 1, k],
                recv_sem=xr_sem.at[d - 1, k],
                device_id={"chan": lax.rem(chan + d, n_chan)},
                device_id_type=MESH,
            )
            token_sends[d, k].start()

    def project(d, k):
        loads[d, k].wait()
        part = pl.ds(k * fc, fc)
        x = tokens[:, part] if d == 0 else xt[d - 1, :, part]
        for j in range(3):
            term = dot(x, wv[d, j, part, :])
            if d == 0 and k == 0:
                acc[j] = term
            else:
                acc[j] += term

    for k in range(parts):
        project(0, k)

    length = toep.shape[2]
    groups = toep.shape[0]
    first_group = seq * piece // gs
    later = lax.broadcasted_iota(jnp.int32, (rows, rows), 1) >= lax.broadcasted_iota(
        jnp.int32, (rows, rows), 0
    )
    for g in range(groups):
        row = filters[pl.ds(first_group + g, 1), :].astype(BF).astype(F32)
        spread = jnp.broadcast_to(row, (rows, length))
        turned = pltpu.roll(spread, 0, 1, stride=1, stride_axis=0)
        toep[g, :, rows:] = turned[:, rows:].astype(BF)
        toep[g, :, :rows] = jnp.where(later, turned[:, :rows], 0.0).astype(BF)

    for k in range(parts):
        for d in range(1, n_chan):
            token_sends[d, k].wait_recv()
            project(d, k)

    for j in range(3):
        ext[j, HALO:, :] = acc[j].astype(BF).astype(F32)
        hs[2 * j : 2 * j + 2, :] = ext[j, HALO + rows - 2 :, :]
    halo = pltpu.make_async_remote_copy(
        src_ref=hs,
        dst_ref=hr,
        send_sem=h_sem.at[0],
        recv_sem=h_sem.at[1],
        device_id={"seq": lax.rem(seq + 1, n_seq)},
        device_id_type=MESH,
    )
    halo.start()
    halo.wait()
    has_past = seq > 0
    for j in range(3):
        ext[j, HALO - 2 : HALO, :] = jnp.where(has_past, hr[2 * j : 2 * j + 2, :], 0.0)

    def stream(j, cols):
        value = taps[j : j + 1, cols] * ext[j, HALO:, cols]
        value = value + taps[3 + j : 4 + j, cols] * ext[j, HALO - 1 : HALO - 1 + rows, cols]
        return value + taps[6 + j : 7 + j, cols] * ext[j, HALO - 2 : HALO - 2 + rows, cols]

    per = LANES // piece
    for b in range(width // LANES):
        cols = pl.ds(b * LANES, LANES)
        z = (stream(1, cols) * stream(2, cols)).astype(BF).astype(F32)
        gated[:, cols] = z
        turned = z.T.reshape(per, piece, rows)
        if padded > piece:
            fill = jnp.zeros((per, padded - piece, rows), F32)
            turned = jnp.concatenate([turned, fill], axis=1)
        zs[b * per : (b + 1) * per] = turned.astype(BF)

    def exchange(source, target, send, recv):
        copies = []
        for d in range(1, n_seq):
            other = lax.rem(seq + d, n_seq)
            copies.append(
                pltpu.make_async_remote_copy(
                    src_ref=source.at[other],
                    dst_ref=target.at[seq],
                    send_sem=send.at[d - 1],
                    recv_sem=recv.at[d - 1],
                    device_id={"seq": other},
                    device_id_type=MESH,
                )
            )
            copies[-1].start()
        target[seq] = source[seq]
        return copies

    z_copies = exchange(zs, zr, z_send, z_recv)
    for b in range(width // LANES):
        cols = pl.ds(b * LANES, LANES)
        first[:, cols] = stream(0, cols)
    for copy in z_copies:
        copy.wait()

    wide = padded // groups
    lags = 2 if n_seq % 2 == 0 else 1
    for g in range(groups):
        x = zr[:, g * wide : (g + 1) * wide, :].reshape(n_seq * wide, rows)
        total = None
        for e in range(0, n_seq, lags):
            rest = (n_seq - e) * wide
            both = dot(x[:rest], toep[g, :, e * rows : (e + lags) * rows])
            for i in range(lags):
                held = (n_seq - e - i) * wide
                term = both[:held, i * rows : (i + 1) * rows]
                if e + i:
                    term = jnp.concatenate(
                        [jnp.zeros(((e + i) * wide, rows), F32), term], axis=0
                    )
                total = term if total is None else total + term
        ys[:, g * wide : (g + 1) * wide, :] = total.astype(BF).reshape(n_seq, wide, rows)

    for copy in exchange(ys, lr, y_send, y_recv):
        copy.wait()

    mixers = []
    for b in range(width // LANES):
        cols = pl.ds(b * LANES, LANES)
        turned = lr[b * per : (b + 1) * per].astype(F32)[:, :piece, :]
        filtered = turned.reshape(LANES, rows).T
        long_out = filtered + skip[:, cols] * gated[:, cols]
        mixers.append((first[:, cols] * long_out).astype(BF))
    mixer = jnp.concatenate(mixers, axis=1)

    part_sends = []
    for d in range(1, n_chan):
        out_loads[d].wait()
        for k in range(parts):
            part = pl.ds(k * fc, fc)
            ps[d - 1, :, part] = dot(mixer, wov[d, :, part]).astype(BF)
            copy = pltpu.make_async_remote_copy(
                src_ref=ps.at[d - 1, :, part],
                dst_ref=pr.at[d - 1, :, part],
                send_sem=p_send.at[d - 1, k],
                recv_sem=p_recv.at[d - 1, k],
                device_id={"chan": lax.rem(chan + d, n_chan)},
                device_id_type=MESH,
            )
            copy.start()
            part_sends.append((d, k, copy))
    out_loads[0].wait()
    sums = []
    for k in range(parts):
        part = pl.ds(k * fc, fc)
        sums.append(dot(mixer, wov[0, :, part]).astype(BF).astype(F32))
    for d, k, copy in part_sends:
        copy.wait_recv()
        part = pl.ds(k * fc, fc)
        sums[k] = sums[k] + pr[d - 1, :, part].astype(F32)
        if d == n_chan - 1:
            out[:, part] = sums[k].astype(BF)
    for d, k, copy in part_sends:
        copy.wait_send()
    for copy in token_sends.values():
        copy.wait_send()


def shards(n_seq, n_chan, tokens, w_in, short_taps, skip_gain, filters, w_out):
    rows, feats = tokens.shape
    width = w_in.shape[2]
    length = filters.shape[1]
    piece = width // n_seq
    gs = width // filters.shape[0]
    padded = max(piece, 16)
    groups = max(piece // gs, 1)
    fc = min(feats, 512)
    parts = feats // fc
    others = max(n_chan - 1, 1)
    vmem = pl.BlockSpec(memory_space=pltpu.VMEM)
    hbm = pl.BlockSpec(memory_space=pl.ANY)
    sem = pltpu.SemaphoreType.DMA
    return pl.pallas_call(
        functools.partial(kernel, n_seq, n_chan, piece, padded, gs, fc),
        out_shape=jax.ShapeDtypeStruct((rows, feats), BF),
        in_specs=[vmem, vmem, vmem, vmem, hbm, hbm],
        out_specs=vmem,
        scratch_shapes=[
            pltpu.VMEM((n_chan, 3, feats, width), BF),
            pltpu.VMEM((n_chan, width, feats), BF),
            pltpu.VMEM((others, rows, feats), BF),
            pltpu.VMEM((3, rows, width), F32),
            pltpu.VMEM((3, HALO + rows, width), F32),
            pltpu.VMEM((rows, width), F32),
            pltpu.VMEM((rows, width), F32),
            pltpu.VMEM((groups, rows, length), BF),
            pltpu.VMEM((n_seq, padded, rows), BF),
            pltpu.VMEM((n_seq, padded, rows), BF),
            pltpu.VMEM((n_seq, padded, rows), BF),
            pltpu.VMEM((n_seq, padded, rows), BF),
            pltpu.VMEM((HALO, width), F32),
            pltpu.VMEM((HALO, width), F32),
            pltpu.VMEM((others, rows, feats), BF),
            pltpu.VMEM((others, rows, feats), BF),
            sem((n_chan, parts)),
            sem((n_chan,)),
            sem((others, parts)),
            sem((others, parts)),
            sem((2,)),
            sem((n_seq,)),
            sem((n_seq,)),
            sem((n_seq,)),
            sem((n_seq,)),
            sem((others, parts)),
            sem((others, parts)),
        ],
        compiler_params=pltpu.CompilerParams(
            collective_id=0, has_side_effects=True, vmem_limit_bytes=58 * 1024 * 1024
        ),
    )(
        tokens,
        short_taps.reshape(9, width),
        skip_gain.reshape(1, width),
        filters,
        jnp.transpose(w_in, (1, 0, 2)),
        w_out,
    )


def solution(mesh):
    placed = (
        P("seq", "chan"),
        P(None, None, "chan"),
        P(None, None, "chan"),
        P("chan"),
        P("chan", None),
        P("chan", None),
    )
    return jax.shard_map(
        functools.partial(shards, mesh.shape["seq"], mesh.shape["chan"]),
        mesh=mesh,
        in_specs=placed,
        out_specs=P("seq", "chan"),
        check_vma=False,
    )
```

```python
import functools

import jax
import jax.numpy as jnp
from jax import lax
from jax.experimental import pallas as pl
from jax.experimental.pallas import tpu as pltpu
from jax.sharding import PartitionSpec as P

MESH = pl.DeviceIdType.MESH
BF = jnp.bfloat16
F32 = jnp.float32
LANES = 128
HALO = 8


def dot(a, b):
    return jnp.dot(a, b, preferred_element_type=F32)


def kernel(
    n_seq, n_chan, halves, piece, padded, gs, fc, fo,
    tokens, taps, skip, filters, w_in, w_out,
    out,
    tv, fv, wv, wov, xt, acc, ext, gated, first, toep, zs, zr, ys, lr, hs, hr, ps, pr,
    w_sem, wo_sem, l_sem, xs_sem, xr_sem, h_send, h_recv,
    z_send, z_recv, y_send, y_recv, p_send, p_recv,
):
    rows, feats = tv.shape
    width = wv.shape[3]
    half = width // halves
    parts = feats // fc
    seq, chan = lax.axis_index("seq"), lax.axis_index("chan")

    def load(d, k):
        source = lax.rem(chan - d + n_chan, n_chan)
        start = pl.multiple_of(source * feats + k * fc, fc)
        return pltpu.make_async_copy(
            w_in.at[:, pl.ds(start, fc), :],
            wv.at[d, :, pl.ds(k * fc, fc), :],
            w_sem.at[d, k],
        )

    def out_load(d):
        target = lax.rem(chan + d, n_chan)
        start = pl.multiple_of(target * feats, feats)
        return pltpu.make_async_copy(
            w_out.at[:, pl.ds(start, feats)], wov.at[d], wo_sem.at[d]
        )

    barrier = pltpu.get_barrier_semaphore()
    for d in range(1, n_chan):
        pl.semaphore_signal(
            barrier, inc=1, device_id={"chan": lax.rem(chan + d, n_chan)}, device_id_type=MESH
        )
    for d in range(1, n_seq):
        pl.semaphore_signal(
            barrier, inc=1, device_id={"seq": lax.rem(seq + d, n_seq)}, device_id_type=MESH
        )
    token_load = pltpu.make_async_copy(tokens, tv, l_sem.at[0])
    token_load.start()
    early = min(2, parts)
    for k in range(early):
        load(0, k).start()
    token_load.wait()
    pl.semaphore_wait(barrier, n_chan - 1 + n_seq - 1)

    token_sends = {}
    for k in range(parts):
        for d in range(1, n_chan):
            token_sends[d, k] = pltpu.make_async_remote_copy(
                src_ref=tv.at[:, pl.ds(k * fc, fc)],
                dst_ref=xt.at[d - 1, :, pl.ds(k * fc, fc)],
                send_sem=xs_sem.at[d - 1, k],
                recv_sem=xr_sem.at[d - 1, k],
                device_id={"chan": lax.rem(chan + d, n_chan)},
                device_id_type=MESH,
            )
            token_sends[d, k].start()
    for k in range(early, parts):
        load(0, k).start()
    filter_load = pltpu.make_async_copy(filters, fv, l_sem.at[1])
    filter_load.start()

    def project(d, k, cols):
        part = pl.ds(k * fc, fc)
        x = tv[:, part] if d == 0 else xt[d - 1, :, part]
        for j in range(3):
            term = dot(x, wv[d, j, part, cols])
            if d == 0 and k == 0:
                acc[j, :, cols] = term
            else:
                acc[j, :, cols] += term

    every = pl.ds(0, width)
    for k in range(parts):
        load(0, k).wait()
        for d in range(1, n_chan):
            load(d, k).start()
        project(0, k, every)

    length = toep.shape[3]
    groups = toep.shape[1]
    later = lax.broadcasted_iota(jnp.int32, (rows, rows), 1) >= lax.broadcasted_iota(
        jnp.int32, (rows, rows), 0
    )
    filter_load.wait()
    for h in range(halves):
        first_group = h * (half // gs) + seq * piece // gs
        for g in range(groups):
            row = fv[pl.ds(first_group + g, 1), :].astype(BF).astype(F32)
            spread = jnp.broadcast_to(row, (rows, length))
            turned = pltpu.roll(spread, 0, 1, stride=1, stride_axis=0)
            toep[h, g, :, rows:] = turned[:, rows:].astype(BF)
            toep[h, g, :, :rows] = jnp.where(later, turned[:, :rows], 0.0).astype(BF)

    sections = [pl.ds(h * half, half) for h in range(halves)]
    halos = []
    for k in range(parts):
        for d in range(1, n_chan):
            load(d, k).wait()
            token_sends[d, k].wait_recv()
            if k < parts - 1 or d < n_chan - 1:
                project(d, k, every)
    for h, cols in enumerate(sections):
        project(n_chan - 1, parts - 1, cols)
        for j in range(3):
            ext[j, HALO:, cols] = acc[j, :, cols].astype(BF).astype(F32)
            hs[h, 2 * j : 2 * j + 2, :] = ext[j, HALO + rows - 2 :, cols]
        halos.append(
            pltpu.make_async_remote_copy(
                src_ref=hs.at[h],
                dst_ref=hr.at[h],
                send_sem=h_send.at[h],
                recv_sem=h_recv.at[h],
                device_id={"seq": lax.rem(seq + 1, n_seq)},
                device_id_type=MESH,
            )
        )
        halos[-1].start()

    for d in list(range(1, n_chan)) + [0]:
        out_load(d).start()

    def stream(j, cols):
        value = taps[0, j : j + 1, cols] * ext[j, HALO:, cols]
        value = value + taps[1, j : j + 1, cols] * ext[j, HALO - 1 : HALO - 1 + rows, cols]
        return value + taps[2, j : j + 1, cols] * ext[j, HALO - 2 : HALO - 2 + rows, cols]

    def exchange(source, target, send, recv):
        copies = []
        for d in range(1, n_seq):
            other = lax.rem(seq + d, n_seq)
            copies.append(
                pltpu.make_async_remote_copy(
                    src_ref=source.at[other],
                    dst_ref=target.at[seq],
                    send_sem=send.at[d - 1],
                    recv_sem=recv.at[d - 1],
                    device_id={"seq": other},
                    device_id_type=MESH,
                )
            )
            copies[-1].start()
        target[seq] = source[seq]
        return copies

    has_past = seq > 0
    per = LANES // piece
    tiles = half // LANES
    z_copies, y_copies = [], []
    for h, cols in enumerate(sections):
        halos[h].wait()
        for j in range(3):
            ext[j, HALO - 2 : HALO, cols] = jnp.where(has_past, hr[h, 2 * j : 2 * j + 2, :], 0.0)
        for b in range(tiles):
            cols = pl.ds(h * half + b * LANES, LANES)
            z = (stream(1, cols) * stream(2, cols)).astype(BF).astype(F32)
            gated[:, cols] = z
            turned = z.T.reshape(per, piece, rows)
            if padded > piece:
                fill = jnp.zeros((per, padded - piece, rows), F32)
                turned = jnp.concatenate([turned, fill], axis=1)
            zs[h, b * per : (b + 1) * per] = turned.astype(BF)
        z_copies.append(exchange(zs.at[h], zr.at[h], z_send.at[h], z_recv.at[h]))
    for b in range(width // LANES):
        cols = pl.ds(b * LANES, LANES)
        first[:, cols] = stream(0, cols)

    wide = padded // groups
    lags = 2 if n_seq % 2 == 0 else 1
    for h in range(halves):
        for copy in z_copies[h]:
            copy.wait_recv()
        for g in range(groups):
            x = zr[h, :, g * wide : (g + 1) * wide, :].reshape(n_seq * wide, rows)
            total = None
            for e in range(0, n_seq, lags):
                rest = (n_seq - e) * wide
                both = dot(x[:rest], toep[h, g, :, e * rows : (e + lags) * rows])
                for i in range(lags):
                    held = (n_seq - e - i) * wide
                    term = both[:held, i * rows : (i + 1) * rows]
                    if e + i:
                        term = jnp.concatenate(
                            [jnp.zeros(((e + i) * wide, rows), F32), term], axis=0
                        )
                    total = term if total is None else total + term
            ys[h, :, g * wide : (g + 1) * wide, :] = total.astype(BF).reshape(n_seq, wide, rows)
        y_copies.append(exchange(ys.at[h], lr.at[h], y_send.at[h], y_recv.at[h]))

    mixers = []
    for h in range(halves):
        for copy in y_copies[h]:
            copy.wait_recv()
        for b in range(tiles):
            cols = pl.ds(h * half + b * LANES, LANES)
            turned = lr[h, b * per : (b + 1) * per].astype(F32)[:, :piece, :]
            filtered = turned.reshape(LANES, rows).T
            long_out = filtered + skip[:, cols] * gated[:, cols]
            mixers.append((first[:, cols] * long_out).astype(BF))
    mixer = jnp.concatenate(mixers, axis=1)

    part_sends = []
    for d in range(1, n_chan):
        out_load(d).wait()
        for k in range(feats // fo):
            part = pl.ds(k * fo, fo)
            ps[d - 1, :, part] = dot(mixer, wov[d, :, part]).astype(BF)
            copy = pltpu.make_async_remote_copy(
                src_ref=ps.at[d - 1, :, part],
                dst_ref=pr.at[d - 1, :, part],
                send_sem=p_send.at[d - 1, k],
                recv_sem=p_recv.at[d - 1, k],
                device_id={"chan": lax.rem(chan + d, n_chan)},
                device_id_type=MESH,
            )
            copy.start()
            part_sends.append((d, k, copy))
    out_load(0).wait()
    sums = []
    for k in range(feats // fo):
        part = pl.ds(k * fo, fo)
        sums.append(dot(mixer, wov[0, :, part]).astype(BF).astype(F32))
    for copies in z_copies + y_copies:
        for copy in copies:
            copy.wait_send()
    for copy in token_sends.values():
        copy.wait_send()
    for d, k, copy in part_sends:
        copy.wait_recv()
        part = pl.ds(k * fo, fo)
        sums[k] = sums[k] + pr[d - 1, :, part].astype(F32)
        if d == n_chan - 1:
            out[:, part] = sums[k].astype(BF)
    for d, k, copy in part_sends:
        copy.wait_send()


def shards(n_seq, n_chan, tokens, w_in, short_taps, skip_gain, filters, w_out):
    rows, feats = tokens.shape
    width = w_in.shape[2]
    length = filters.shape[1]
    gs = width // filters.shape[0]
    halves = 2 if width % (2 * n_seq * gs) == 0 else 1
    half = width // halves
    piece = half // n_seq
    padded = max(piece, 16)
    groups = max(piece // gs, 1)
    fc = min(feats, 512)
    fo = min(feats, 256)
    parts, cuts = feats // fc, feats // fo
    others = max(n_chan - 1, 1)
    vmem = pl.BlockSpec(memory_space=pltpu.VMEM)
    hbm = pl.BlockSpec(memory_space=pl.ANY)
    sem = pltpu.SemaphoreType.DMA
    return pl.pallas_call(
        functools.partial(kernel, n_seq, n_chan, halves, piece, padded, gs, fc, fo),
        out_shape=jax.ShapeDtypeStruct((rows, feats), BF),
        in_specs=[hbm, vmem, vmem, hbm, hbm, hbm],
        out_specs=vmem,
        scratch_shapes=[
            pltpu.VMEM((rows, feats), BF),
            pltpu.VMEM(filters.shape, F32),
            pltpu.VMEM((n_chan, 3, feats, width), BF),
            pltpu.VMEM((n_chan, width, feats), BF),
            pltpu.VMEM((others, rows, feats), BF),
            pltpu.VMEM((3, rows, width), F32),
            pltpu.VMEM((3, HALO + rows, width), F32),
            pltpu.VMEM((rows, width), F32),
            pltpu.VMEM((rows, width), F32),
            pltpu.VMEM((halves, groups, rows, length), BF),
            pltpu.VMEM((halves, n_seq, padded, rows), BF),
            pltpu.VMEM((halves, n_seq, padded, rows), BF),
            pltpu.VMEM((halves, n_seq, padded, rows), BF),
            pltpu.VMEM((halves, n_seq, padded, rows), BF),
            pltpu.VMEM((halves, HALO, half), F32),
            pltpu.VMEM((halves, HALO, half), F32),
            pltpu.VMEM((others, rows, feats), BF),
            pltpu.VMEM((others, rows, feats), BF),
            sem((n_chan, parts)),
            sem((n_chan,)),
            sem((2,)),
            sem((others, parts)),
            sem((others, parts)),
            sem((halves,)),
            sem((halves,)),
            sem((halves, n_seq)),
            sem((halves, n_seq)),
            sem((halves, n_seq)),
            sem((halves, n_seq)),
            sem((others, cuts)),
            sem((others, cuts)),
        ],
        compiler_params=pltpu.CompilerParams(
            collective_id=0, has_side_effects=True, vmem_limit_bytes=58 * 1024 * 1024
        ),
    )(
        tokens,
        short_taps,
        skip_gain.reshape(1, width),
        filters,
        jnp.transpose(w_in, (1, 0, 2)),
        w_out,
    )


def solution(mesh):
    placed = (
        P("seq", "chan"),
        P(None, None, "chan"),
        P(None, None, "chan"),
        P("chan"),
        P("chan", None),
        P("chan", None),
    )
    return jax.shard_map(
        functools.partial(shards, mesh.shape["seq"], mesh.shape["chan"]),
        mesh=mesh,
        in_specs=placed,
        out_specs=P("seq", "chan"),
        check_vma=False,
    )
```

```python
import functools

import jax
import jax.numpy as jnp
from jax import lax
from jax.experimental import pallas as pl
from jax.experimental.pallas import tpu as pltpu
from jax.sharding import PartitionSpec as P

MESH = pl.DeviceIdType.MESH
BF = jnp.bfloat16
F32 = jnp.float32
LANES = 128
HALO = 8


def dot(a, b):
    return jnp.dot(a, b, preferred_element_type=F32)


def kernel(
    n_seq, n_chan, halves, piece, padded, gs, fc, fo,
    tokens, taps, skip, filters, w_in, w_out,
    out,
    tv, fv, wv, wov, xt, acc, ext, gated, first, toep, zs, zr, ys, lr, hs, hr, ps, pr,
    w_sem, wo_sem, l_sem, xs_sem, xr_sem, h_send, h_recv,
    z_send, z_recv, y_send, y_recv, p_send, p_recv, rounds,
):
    rows, feats = tv.shape
    width = wv.shape[3]
    half = width // halves
    parts = feats // fc
    seq, chan = lax.axis_index("seq"), lax.axis_index("chan")

    def load(d, k):
        source = lax.rem(chan - d + n_chan, n_chan)
        start = pl.multiple_of(source * feats + k * fc, fc)
        return pltpu.make_async_copy(
            w_in.at[:, pl.ds(start, fc), :],
            wv.at[d, :, pl.ds(k * fc, fc), :],
            w_sem.at[d, k],
        )

    def out_load(d):
        target = lax.rem(chan + d, n_chan)
        start = pl.multiple_of(target * feats, feats)
        return pltpu.make_async_copy(
            w_out.at[:, pl.ds(start, feats)], wov.at[d], wo_sem.at[d]
        )

    barrier = pltpu.get_barrier_semaphore()
    for d in range(1, n_chan):
        pl.semaphore_signal(
            barrier, inc=1, device_id={"chan": lax.rem(chan + d, n_chan)}, device_id_type=MESH
        )
    pairs = []
    bit = 1
    while bit < n_seq:
        pairs.append(seq + bit * (1 - 2 * lax.rem(lax.div(seq, bit), 2)))
        bit *= 2
    for other in pairs:
        pl.semaphore_signal(barrier, inc=1, device_id={"seq": other}, device_id_type=MESH)
    token_load = pltpu.make_async_copy(tokens, tv, l_sem.at[0])
    token_load.start()
    early = min(2, parts)
    for k in range(early):
        load(0, k).start()
    token_load.wait()
    pl.semaphore_wait(barrier, n_chan - 1 + len(pairs))

    token_sends = {}
    for k in range(parts):
        for d in range(1, n_chan):
            token_sends[d, k] = pltpu.make_async_remote_copy(
                src_ref=tv.at[:, pl.ds(k * fc, fc)],
                dst_ref=xt.at[d - 1, :, pl.ds(k * fc, fc)],
                send_sem=xs_sem.at[d - 1, k],
                recv_sem=xr_sem.at[d - 1, k],
                device_id={"chan": lax.rem(chan + d, n_chan)},
                device_id_type=MESH,
            )
            token_sends[d, k].start()
    for k in range(early, parts):
        load(0, k).start()
    filter_load = pltpu.make_async_copy(filters, fv, l_sem.at[1])
    filter_load.start()

    def project(d, k, cols):
        part = pl.ds(k * fc, fc)
        x = tv[:, part] if d == 0 else xt[d - 1, :, part]
        for j in range(3):
            term = dot(x, wv[d, j, part, cols])
            if d == 0 and k == 0:
                acc[j, :, cols] = term
            else:
                acc[j, :, cols] += term

    def round_signal(i):
        if i < len(pairs):
            pl.semaphore_signal(
                rounds.at[i], inc=1, device_id={"seq": pairs[i]}, device_id_type=MESH
            )

    def round_end(i):
        if i < len(pairs):
            pl.semaphore_wait(rounds.at[i], 1)
            round_signal(i + 1)

    every = pl.ds(0, width)
    round_signal(0)
    for k in range(parts):
        load(0, k).wait()
        for d in range(1, n_chan):
            load(d, k).start()
        project(0, k, every)
        round_end(k)
    for k in range(parts, len(pairs)):
        round_end(k)

    length = toep.shape[3]
    groups = toep.shape[1]
    later = lax.broadcasted_iota(jnp.int32, (rows, rows), 1) >= lax.broadcasted_iota(
        jnp.int32, (rows, rows), 0
    )
    filter_load.wait()
    for h in range(halves):
        first_group = h * (half // gs) + seq * piece // gs
        for g in range(groups):
            row = fv[pl.ds(first_group + g, 1), :].astype(BF).astype(F32)
            spread = jnp.broadcast_to(row, (rows, length))
            turned = pltpu.roll(spread, 0, 1, stride=1, stride_axis=0)
            toep[h, g, :, rows:] = turned[:, rows:].astype(BF)
            toep[h, g, :, :rows] = jnp.where(later, turned[:, :rows], 0.0).astype(BF)

    sections = [pl.ds(h * half, half) for h in range(halves)]
    halos = []
    for k in range(parts):
        for d in range(1, n_chan):
            load(d, k).wait()
            token_sends[d, k].wait_recv()
            if k < parts - 1 or d < n_chan - 1:
                project(d, k, every)
    for h, cols in enumerate(sections):
        project(n_chan - 1, parts - 1, cols)
        for j in range(3):
            ext[j, HALO:, cols] = acc[j, :, cols].astype(BF).astype(F32)
            hs[h, 2 * j : 2 * j + 2, :] = ext[j, HALO + rows - 2 :, cols]
        halos.append(
            pltpu.make_async_remote_copy(
                src_ref=hs.at[h],
                dst_ref=hr.at[h],
                send_sem=h_send.at[h],
                recv_sem=h_recv.at[h],
                device_id={"seq": lax.rem(seq + 1, n_seq)},
                device_id_type=MESH,
            )
        )
        halos[-1].start()

    for d in list(range(1, n_chan)) + [0]:
        out_load(d).start()

    def stream(j, cols):
        value = taps[0, j : j + 1, cols] * ext[j, HALO:, cols]
        value = value + taps[1, j : j + 1, cols] * ext[j, HALO - 1 : HALO - 1 + rows, cols]
        return value + taps[2, j : j + 1, cols] * ext[j, HALO - 2 : HALO - 2 + rows, cols]

    def exchange(source, target, send, recv):
        copies = []
        for d in range(1, n_seq):
            other = lax.rem(seq + d, n_seq)
            copies.append(
                pltpu.make_async_remote_copy(
                    src_ref=source.at[other],
                    dst_ref=target.at[seq],
                    send_sem=send.at[d - 1],
                    recv_sem=recv.at[d - 1],
                    device_id={"seq": other},
                    device_id_type=MESH,
                )
            )
            copies[-1].start()
        target[seq] = source[seq]
        return copies

    has_past = seq > 0
    per = LANES // piece
    tiles = half // LANES
    z_copies, y_copies = [], []
    for h, cols in enumerate(sections):
        halos[h].wait()
        for j in range(3):
            ext[j, HALO - 2 : HALO, cols] = jnp.where(has_past, hr[h, 2 * j : 2 * j + 2, :], 0.0)
        for b in range(tiles):
            cols = pl.ds(h * half + b * LANES, LANES)
            z = (stream(1, cols) * stream(2, cols)).astype(BF).astype(F32)
            gated[:, cols] = z
            turned = z.T.reshape(per, piece, rows)
            if padded > piece:
                fill = jnp.zeros((per, padded - piece, rows), F32)
                turned = jnp.concatenate([turned, fill], axis=1)
            zs[h, b * per : (b + 1) * per] = turned.astype(BF)
        z_copies.append(exchange(zs.at[h], zr.at[h], z_send.at[h], z_recv.at[h]))
    for b in range(width // LANES):
        cols = pl.ds(b * LANES, LANES)
        first[:, cols] = stream(0, cols)

    wide = padded // groups
    lags = 2 if n_seq % 2 == 0 else 1
    for h in range(halves):
        for copy in z_copies[h]:
            copy.wait_recv()
        for g in range(groups):
            x = zr[h, :, g * wide : (g + 1) * wide, :].reshape(n_seq * wide, rows)
            total = None
            for e in range(0, n_seq, lags):
                rest = (n_seq - e) * wide
                both = dot(x[:rest], toep[h, g, :, e * rows : (e + lags) * rows])
                for i in range(lags):
                    held = (n_seq - e - i) * wide
                    term = both[:held, i * rows : (i + 1) * rows]
                    if e + i:
                        term = jnp.concatenate(
                            [jnp.zeros(((e + i) * wide, rows), F32), term], axis=0
                        )
                    total = term if total is None else total + term
            ys[h, :, g * wide : (g + 1) * wide, :] = total.astype(BF).reshape(n_seq, wide, rows)
        y_copies.append(exchange(ys.at[h], lr.at[h], y_send.at[h], y_recv.at[h]))

    mixers = []
    for h in range(halves):
        for copy in y_copies[h]:
            copy.wait_recv()
        for b in range(tiles):
            cols = pl.ds(h * half + b * LANES, LANES)
            turned = lr[h, b * per : (b + 1) * per].astype(F32)[:, :piece, :]
            filtered = turned.reshape(LANES, rows).T
            long_out = filtered + skip[:, cols] * gated[:, cols]
            mixers.append((first[:, cols] * long_out).astype(BF))
    mixer = jnp.concatenate(mixers, axis=1)

    part_sends = []
    for d in range(1, n_chan):
        out_load(d).wait()
        for k in range(feats // fo):
            part = pl.ds(k * fo, fo)
            ps[d - 1, :, part] = dot(mixer, wov[d, :, part]).astype(BF)
            copy = pltpu.make_async_remote_copy(
                src_ref=ps.at[d - 1, :, part],
                dst_ref=pr.at[d - 1, :, part],
                send_sem=p_send.at[d - 1, k],
                recv_sem=p_recv.at[d - 1, k],
                device_id={"chan": lax.rem(chan + d, n_chan)},
                device_id_type=MESH,
            )
            copy.start()
            part_sends.append((d, k, copy))
    out_load(0).wait()
    sums = []
    for k in range(feats // fo):
        part = pl.ds(k * fo, fo)
        sums.append(dot(mixer, wov[0, :, part]).astype(BF).astype(F32))
    for copies in z_copies + y_copies:
        for copy in copies:
            copy.wait_send()
    for copy in token_sends.values():
        copy.wait_send()
    for d, k, copy in part_sends:
        copy.wait_recv()
        part = pl.ds(k * fo, fo)
        sums[k] = sums[k] + pr[d - 1, :, part].astype(F32)
        if d == n_chan - 1:
            out[:, part] = sums[k].astype(BF)
    for d, k, copy in part_sends:
        copy.wait_send()


def shards(n_seq, n_chan, tokens, w_in, short_taps, skip_gain, filters, w_out):
    rows, feats = tokens.shape
    width = w_in.shape[2]
    length = filters.shape[1]
    gs = width // filters.shape[0]
    halves = 2 if width % (2 * n_seq * gs) == 0 else 1
    half = width // halves
    piece = half // n_seq
    padded = max(piece, 16)
    groups = max(piece // gs, 1)
    fc = min(feats, 512)
    fo = min(feats, 256)
    parts, cuts = feats // fc, feats // fo
    others = max(n_chan - 1, 1)
    vmem = pl.BlockSpec(memory_space=pltpu.VMEM)
    hbm = pl.BlockSpec(memory_space=pl.ANY)
    sem = pltpu.SemaphoreType.DMA
    return pl.pallas_call(
        functools.partial(kernel, n_seq, n_chan, halves, piece, padded, gs, fc, fo),
        out_shape=jax.ShapeDtypeStruct((rows, feats), BF),
        in_specs=[hbm, vmem, vmem, hbm, hbm, hbm],
        out_specs=vmem,
        scratch_shapes=[
            pltpu.VMEM((rows, feats), BF),
            pltpu.VMEM(filters.shape, F32),
            pltpu.VMEM((n_chan, 3, feats, width), BF),
            pltpu.VMEM((n_chan, width, feats), BF),
            pltpu.VMEM((others, rows, feats), BF),
            pltpu.VMEM((3, rows, width), F32),
            pltpu.VMEM((3, HALO + rows, width), F32),
            pltpu.VMEM((rows, width), F32),
            pltpu.VMEM((rows, width), F32),
            pltpu.VMEM((halves, groups, rows, length), BF),
            pltpu.VMEM((halves, n_seq, padded, rows), BF),
            pltpu.VMEM((halves, n_seq, padded, rows), BF),
            pltpu.VMEM((halves, n_seq, padded, rows), BF),
            pltpu.VMEM((halves, n_seq, padded, rows), BF),
            pltpu.VMEM((halves, HALO, half), F32),
            pltpu.VMEM((halves, HALO, half), F32),
            pltpu.VMEM((others, rows, feats), BF),
            pltpu.VMEM((others, rows, feats), BF),
            sem((n_chan, parts)),
            sem((n_chan,)),
            sem((2,)),
            sem((others, parts)),
            sem((others, parts)),
            sem((halves,)),
            sem((halves,)),
            sem((halves, n_seq)),
            sem((halves, n_seq)),
            sem((halves, n_seq)),
            sem((halves, n_seq)),
            sem((others, cuts)),
            sem((others, cuts)),
            pltpu.SemaphoreType.REGULAR((n_seq.bit_length(),)),
        ],
        compiler_params=pltpu.CompilerParams(
            collective_id=0, has_side_effects=True, vmem_limit_bytes=58 * 1024 * 1024
        ),
    )(
        tokens,
        short_taps,
        skip_gain.reshape(1, width),
        filters,
        jnp.transpose(w_in, (1, 0, 2)),
        w_out,
    )


def solution(mesh):
    placed = (
        P("seq", "chan"),
        P(None, None, "chan"),
        P(None, None, "chan"),
        P("chan"),
        P("chan", None),
        P("chan", None),
    )
    return jax.shard_map(
        functools.partial(shards, mesh.shape["seq"], mesh.shape["chan"]),
        mesh=mesh,
        in_specs=placed,
        out_specs=P("seq", "chan"),
        check_vma=False,
    )
```

```python
import functools

import jax
import jax.numpy as jnp
from jax import lax
from jax.experimental import pallas as pl
from jax.experimental.pallas import tpu as pltpu
from jax.sharding import PartitionSpec as P

MESH = pl.DeviceIdType.MESH
BF = jnp.bfloat16
F32 = jnp.float32
LANES = 128
HALO = 8


def dot(a, b):
    return jnp.dot(a, b, preferred_element_type=F32)


def kernel(
    n_seq, n_chan, halves, piece, padded, gs, fc, fo,
    tokens, taps, skip, filters, w_in, w_out,
    out,
    tv, fv, wv, wov, xt, acc, ext, gated, first, toep, zs, zr, ys, lr, hs, hr, ps, pr,
    w_sem, wo_sem, l_sem, xs_sem, xr_sem, h_send, h_recv,
    z_send, z_recv, y_send, y_recv, p_send, p_recv, rounds,
):
    rows, feats = tv.shape
    width = wv.shape[3]
    half = width // halves
    parts = feats // fc
    seq, chan = lax.axis_index("seq"), lax.axis_index("chan")

    def load(d, k):
        source = lax.rem(chan - d + n_chan, n_chan)
        start = pl.multiple_of(source * feats + k * fc, fc)
        return pltpu.make_async_copy(
            w_in.at[:, pl.ds(start, fc), :],
            wv.at[d, :, pl.ds(k * fc, fc), :],
            w_sem.at[d, k],
        )

    def out_load(d):
        target = lax.rem(chan + d, n_chan)
        start = pl.multiple_of(target * feats, feats)
        return pltpu.make_async_copy(
            w_out.at[:, pl.ds(start, feats)], wov.at[d], wo_sem.at[d]
        )

    barrier = pltpu.get_barrier_semaphore()
    for d in range(1, n_chan):
        pl.semaphore_signal(
            barrier, inc=1, device_id={"chan": lax.rem(chan + d, n_chan)}, device_id_type=MESH
        )
    pairs = []
    bit = 1
    while bit < n_seq:
        pairs.append(seq + bit * (1 - 2 * lax.rem(lax.div(seq, bit), 2)))
        bit *= 2
    for other in pairs:
        pl.semaphore_signal(barrier, inc=1, device_id={"seq": other}, device_id_type=MESH)
    token_load = pltpu.make_async_copy(tokens, tv, l_sem.at[0])
    token_load.start()
    token_load.wait()
    pl.semaphore_wait(barrier, n_chan - 1 + len(pairs))

    token_sends = {}
    for k in range(parts):
        for d in range(1, n_chan):
            token_sends[d, k] = pltpu.make_async_remote_copy(
                src_ref=tv.at[:, pl.ds(k * fc, fc)],
                dst_ref=xt.at[d - 1, :, pl.ds(k * fc, fc)],
                send_sem=xs_sem.at[d - 1, k],
                recv_sem=xr_sem.at[d - 1, k],
                device_id={"chan": lax.rem(chan + d, n_chan)},
                device_id_type=MESH,
            )
            token_sends[d, k].start()
    for k in range(parts):
        load(0, k).start()
    filter_load = pltpu.make_async_copy(filters, fv, l_sem.at[1])
    filter_load.start()

    def project(d, k, cols):
        part = pl.ds(k * fc, fc)
        x = tv[:, part] if d == 0 else xt[d - 1, :, part]
        for j in range(3):
            term = dot(x, wv[d, j, part, cols])
            if d == 0 and k == 0:
                acc[j, :, cols] = term
            else:
                acc[j, :, cols] += term

    def round_signal(i):
        if i < len(pairs):
            pl.semaphore_signal(
                rounds.at[i], inc=1, device_id={"seq": pairs[i]}, device_id_type=MESH
            )

    def round_end(i):
        if i < len(pairs):
            pl.semaphore_wait(rounds.at[i], 1)
            round_signal(i + 1)

    every = pl.ds(0, width)
    round_signal(0)
    for k in range(parts):
        load(0, k).wait()
        for d in range(1, n_chan):
            load(d, k).start()
        project(0, k, every)
        round_end(k)
    for k in range(parts, len(pairs)):
        round_end(k)

    length = toep.shape[3]
    groups = toep.shape[1]
    later = lax.broadcasted_iota(jnp.int32, (rows, rows), 1) >= lax.broadcasted_iota(
        jnp.int32, (rows, rows), 0
    )
    filter_load.wait()
    for h in range(halves):
        first_group = h * (half // gs) + seq * piece // gs
        for g in range(groups):
            row = fv[pl.ds(first_group + g, 1), :].astype(BF).astype(F32)
            spread = jnp.broadcast_to(row, (rows, length))
            turned = pltpu.roll(spread, 0, 1, stride=1, stride_axis=0)
            toep[h, g, :, rows:] = turned[:, rows:].astype(BF)
            toep[h, g, :, :rows] = jnp.where(later, turned[:, :rows], 0.0).astype(BF)

    sections = [pl.ds(h * half, half) for h in range(halves)]
    halos = []
    for k in range(parts):
        for d in range(1, n_chan):
            load(d, k).wait()
            token_sends[d, k].wait_recv()
            if k < parts - 1 or d < n_chan - 1:
                project(d, k, every)
    for h, cols in enumerate(sections):
        project(n_chan - 1, parts - 1, cols)
        for j in range(3):
            ext[j, HALO:, cols] = acc[j, :, cols].astype(BF).astype(F32)
            hs[h, 2 * j : 2 * j + 2, :] = ext[j, HALO + rows - 2 :, cols]
        halos.append(
            pltpu.make_async_remote_copy(
                src_ref=hs.at[h],
                dst_ref=hr.at[h],
                send_sem=h_send.at[h],
                recv_sem=h_recv.at[h],
                device_id={"seq": lax.rem(seq + 1, n_seq)},
                device_id_type=MESH,
            )
        )
        halos[-1].start()

    for d in list(range(1, n_chan)) + [0]:
        out_load(d).start()

    def stream(j, cols):
        value = taps[0, j : j + 1, cols] * ext[j, HALO:, cols]
        value = value + taps[1, j : j + 1, cols] * ext[j, HALO - 1 : HALO - 1 + rows, cols]
        return value + taps[2, j : j + 1, cols] * ext[j, HALO - 2 : HALO - 2 + rows, cols]

    def exchange(source, target, send, recv):
        copies = []
        for d in sorted(range(1, n_seq), key=lambda d: -min(d, n_seq - d)):
            other = lax.rem(seq + d, n_seq)
            copies.append(
                pltpu.make_async_remote_copy(
                    src_ref=source.at[other],
                    dst_ref=target.at[seq],
                    send_sem=send.at[d - 1],
                    recv_sem=recv.at[d - 1],
                    device_id={"seq": other},
                    device_id_type=MESH,
                )
            )
            copies[-1].start()
        target[seq] = source[seq]
        return copies

    has_past = seq > 0
    per = LANES // piece
    tiles = half // LANES
    z_copies, y_copies = [], []
    for h, cols in enumerate(sections):
        halos[h].wait()
        for j in range(3):
            ext[j, HALO - 2 : HALO, cols] = jnp.where(has_past, hr[h, 2 * j : 2 * j + 2, :], 0.0)
        for b in range(tiles):
            cols = pl.ds(h * half + b * LANES, LANES)
            z = (stream(1, cols) * stream(2, cols)).astype(BF).astype(F32)
            gated[:, cols] = z
            turned = z.T.reshape(per, piece, rows)
            if padded > piece:
                fill = jnp.zeros((per, padded - piece, rows), F32)
                turned = jnp.concatenate([turned, fill], axis=1)
            zs[h, b * per : (b + 1) * per] = turned.astype(BF)
        z_copies.append(exchange(zs.at[h], zr.at[h], z_send.at[h], z_recv.at[h]))
    for b in range(width // LANES):
        cols = pl.ds(b * LANES, LANES)
        first[:, cols] = stream(0, cols)

    wide = padded // groups
    lags = 2 if n_seq % 2 == 0 else 1
    for h in range(halves):
        for copy in z_copies[h]:
            copy.wait_recv()
        for g in range(groups):
            x = zr[h, :, g * wide : (g + 1) * wide, :].reshape(n_seq * wide, rows)
            total = None
            for e in range(0, n_seq, lags):
                rest = (n_seq - e) * wide
                both = dot(x[:rest], toep[h, g, :, e * rows : (e + lags) * rows])
                for i in range(lags):
                    held = (n_seq - e - i) * wide
                    term = both[:held, i * rows : (i + 1) * rows]
                    if e + i:
                        term = jnp.concatenate(
                            [jnp.zeros(((e + i) * wide, rows), F32), term], axis=0
                        )
                    total = term if total is None else total + term
            ys[h, :, g * wide : (g + 1) * wide, :] = total.astype(BF).reshape(n_seq, wide, rows)
        y_copies.append(exchange(ys.at[h], lr.at[h], y_send.at[h], y_recv.at[h]))

    mixers = []
    for h in range(halves):
        for copy in y_copies[h]:
            copy.wait_recv()
        for b in range(tiles):
            cols = pl.ds(h * half + b * LANES, LANES)
            turned = lr[h, b * per : (b + 1) * per].astype(F32)[:, :piece, :]
            filtered = turned.reshape(LANES, rows).T
            long_out = filtered + skip[:, cols] * gated[:, cols]
            mixers.append((first[:, cols] * long_out).astype(BF))
    mixer = jnp.concatenate(mixers, axis=1)

    part_sends = []
    for d in range(1, n_chan):
        out_load(d).wait()
        for k in range(feats // fo):
            part = pl.ds(k * fo, fo)
            ps[d - 1, :, part] = dot(mixer, wov[d, :, part]).astype(BF)
            copy = pltpu.make_async_remote_copy(
                src_ref=ps.at[d - 1, :, part],
                dst_ref=pr.at[d - 1, :, part],
                send_sem=p_send.at[d - 1, k],
                recv_sem=p_recv.at[d - 1, k],
                device_id={"chan": lax.rem(chan + d, n_chan)},
                device_id_type=MESH,
            )
            copy.start()
            part_sends.append((d, k, copy))
    out_load(0).wait()
    sums = []
    for k in range(feats // fo):
        part = pl.ds(k * fo, fo)
        sums.append(dot(mixer, wov[0, :, part]).astype(BF).astype(F32))
    for copies in z_copies + y_copies:
        for copy in copies:
            copy.wait_send()
    for copy in token_sends.values():
        copy.wait_send()
    for d, k, copy in part_sends:
        copy.wait_recv()
        part = pl.ds(k * fo, fo)
        sums[k] = sums[k] + pr[d - 1, :, part].astype(F32)
        if d == n_chan - 1:
            out[:, part] = sums[k].astype(BF)
    for d, k, copy in part_sends:
        copy.wait_send()


def shards(n_seq, n_chan, tokens, w_in, short_taps, skip_gain, filters, w_out):
    rows, feats = tokens.shape
    width = w_in.shape[2]
    length = filters.shape[1]
    gs = width // filters.shape[0]
    halves = 2 if width % (2 * n_seq * gs) == 0 else 1
    half = width // halves
    piece = half // n_seq
    padded = max(piece, 16)
    groups = max(piece // gs, 1)
    fc = min(feats, 256)
    fo = min(feats, 256)
    parts, cuts = feats // fc, feats // fo
    others = max(n_chan - 1, 1)
    vmem = pl.BlockSpec(memory_space=pltpu.VMEM)
    hbm = pl.BlockSpec(memory_space=pl.ANY)
    sem = pltpu.SemaphoreType.DMA
    return pl.pallas_call(
        functools.partial(kernel, n_seq, n_chan, halves, piece, padded, gs, fc, fo),
        out_shape=jax.ShapeDtypeStruct((rows, feats), BF),
        in_specs=[hbm, vmem, vmem, hbm, hbm, hbm],
        out_specs=vmem,
        scratch_shapes=[
            pltpu.VMEM((rows, feats), BF),
            pltpu.VMEM(filters.shape, F32),
            pltpu.VMEM((n_chan, 3, feats, width), BF),
            pltpu.VMEM((n_chan, width, feats), BF),
            pltpu.VMEM((others, rows, feats), BF),
            pltpu.VMEM((3, rows, width), F32),
            pltpu.VMEM((3, HALO + rows, width), F32),
            pltpu.VMEM((rows, width), F32),
            pltpu.VMEM((rows, width), F32),
            pltpu.VMEM((halves, groups, rows, length), BF),
            pltpu.VMEM((halves, n_seq, padded, rows), BF),
            pltpu.VMEM((halves, n_seq, padded, rows), BF),
            pltpu.VMEM((halves, n_seq, padded, rows), BF),
            pltpu.VMEM((halves, n_seq, padded, rows), BF),
            pltpu.VMEM((halves, HALO, half), F32),
            pltpu.VMEM((halves, HALO, half), F32),
            pltpu.VMEM((others, rows, feats), BF),
            pltpu.VMEM((others, rows, feats), BF),
            sem((n_chan, parts)),
            sem((n_chan,)),
            sem((2,)),
            sem((others, parts)),
            sem((others, parts)),
            sem((halves,)),
            sem((halves,)),
            sem((halves, n_seq)),
            sem((halves, n_seq)),
            sem((halves, n_seq)),
            sem((halves, n_seq)),
            sem((others, cuts)),
            sem((others, cuts)),
            pltpu.SemaphoreType.REGULAR((n_seq.bit_length(),)),
        ],
        compiler_params=pltpu.CompilerParams(
            collective_id=0, has_side_effects=True, vmem_limit_bytes=58 * 1024 * 1024
        ),
    )(
        tokens,
        short_taps,
        skip_gain.reshape(1, width),
        filters,
        jnp.transpose(w_in, (1, 0, 2)),
        w_out,
    )


def solution(mesh):
    placed = (
        P("seq", "chan"),
        P(None, None, "chan"),
        P(None, None, "chan"),
        P("chan"),
        P("chan", None),
        P("chan", None),
    )
    return jax.shard_map(
        functools.partial(shards, mesh.shape["seq"], mesh.shape["chan"]),
        mesh=mesh,
        in_specs=placed,
        out_specs=P("seq", "chan"),
        check_vma=False,
    )
```
